768 devices in a mesh: node: 16 (over x, z_hi), local: 48 (over z_lo, y, core).
Axes of the slice: x: 4, y: 8, z: 12 (z_hi: 4, z_lo: 3; z = z_hi * 3 + z_lo), core: 2. Of those that a mesh axis runs over, the one named last changes fastest.
Arguments:
- acts: bfloat16 [196608, 6144], P(('node', 'local')), may hold values from -24 to 24
- key_cot: bfloat16 [196608, 512], P(('node', 'local')), may hold values from -0.013671875 to 0.013671875
- value_cot: bfloat16 [196608, 512], P(('node', 'local')), may hold values from -0.013671875 to 0.013671875
Outputs:
- kv_grad: float32 [6144, 1024], P(('node', 'local'))
The draws below stay inside these ranges and needn't reach their ends.
All inputs are finite; a program needn't handle non-finite values.
Results may differ from the reference program's by a relative error of at most 0.01.
Values may be sent and summed in bfloat16 or wider, within the bound.
A program may use at most 64 MiB of HBM per device.

```python
import jax
import jax.numpy as jnp
from jax import lax

D = 6144
KVW = 512
TOK_DEV = 256
TOKENS = 196608
N_NODE = 16
N_LOCAL = 48


def strengthened(entries, key, source, target, blocks, factor):
    def block_of(position):
        return (jnp.arange(entries.shape[position]) // (entries.shape[position] // blocks)).reshape((-1,) + (1,) * (entries.ndim - 1 - position))

    one_side = jax.random.permutation(key, blocks)[block_of(target)]
    far = (block_of(target) + blocks // 2) % blocks
    return jnp.where((block_of(source) == one_side) | (block_of(source) == far), factor * entries, entries)


def block_levels(rng, dims, shards, least, largest):
    loudness, own = 1.0, jax.random.fold_in(rng, 6)
    for position, parts in shards:
        heights = jnp.exp(jax.random.uniform(jax.random.fold_in(own, position), (parts,), jnp.float32, least / len(shards), largest / len(shards)))
        loudness = loudness * jnp.repeat(heights, dims[position] // parts).reshape([-1 if axis == position else 1 for axis in range(len(dims))])
    return loudness


def bell_draw(key, shape, spread, most, split=(), held_as=jnp.bfloat16):
    values = jax.random.normal(key, shape, jnp.float32) * spread
    if len(split) > 0:
        values = block_levels(key, shape, split, -0.22, 0.18) * values
    return jnp.clip(values, min=-most, max=most).astype(held_as)


def bell_draw_with(own_key, extent, width, bound, shards, heavy, kind=jnp.bfloat16):
    entries = width * jax.random.normal(own_key, extent, jnp.float32)
    if shards:
        entries = entries * block_levels(own_key, extent, shards, -0.22, 0.18)
    return jnp.clip(strengthened(entries, jax.random.fold_in(own_key, 3), *heavy), -bound, bound).astype(kind)


def setup_inputs(seed: int = 0) -> dict:
    key_of = jax.random.split(jax.random.key(seed), 4)
    acts = bell_draw_with(key_of[0], (TOKENS, D), 1.0, 24.0, ((0, 768),), (0, 1, 768, 6.0))
    key_cot = bell_draw(key_of[1], (TOKENS, KVW), TOKENS ** -0.5, 0.013671875, ((0, 768),))
    value_cot = bell_draw(key_of[2], (TOKENS, KVW), TOKENS ** -0.5, 0.013671875, ((0, 768),))
    return {"acts": acts, "key_cot": key_cot, "value_cot": value_cot}


def reference(acts, key_cot, value_cot):
    inputs = acts.reshape(N_NODE, N_LOCAL, TOK_DEV, D)
    cotan = jnp.concatenate([key_cot, value_cot], axis=1).reshape(N_NODE, N_LOCAL, TOK_DEV, 2 * KVW)

    def group_sum(pair):
        rows_in, rows_cot = pair

        def add_device(total, item):
            left, right = item
            piece = lax.dot_general(left, right, (((0,), (0,)), ((), ())), preferred_element_type=jnp.float32)
            return total + piece.astype(jnp.bfloat16).astype(jnp.float32), None

        start = jnp.zeros((D, 2 * KVW), jnp.float32)
        total, _ = lax.scan(add_device, start, (rows_in, rows_cot))
        return total.astype(jnp.bfloat16)

    groups = lax.map(group_sum, (inputs, cotan))
    return jnp.sum(groups.astype(jnp.float32), axis=0)
```

```python
import functools

import jax
import jax.numpy as jnp
from jax import lax
from jax.experimental import pallas as pl
from jax.experimental.pallas import tpu as pltpu
from jax.sharding import PartitionSpec as P

MESH = pl.DeviceIdType.MESH
F32, BF16 = jnp.float32, jnp.bfloat16
ROWS = 16


class Torus:
    def __init__(self, n_node, n_local, nx, ny):
        self.nx, self.ny = nx, ny
        self.zh = n_node // nx
        self.zl = n_local // (2 * ny)
        self.nz = self.zh * self.zl

    def here(self):
        node, local = lax.axis_index("node"), lax.axis_index("local")
        x, zh = node // self.zh, node % self.zh
        zl, yc = local // (2 * self.ny), local % (2 * self.ny)
        return x, yc // 2, zh * self.zl + zl, yc % 2

    def device(self, x, y, z, core):
        return (
            x * self.zh + z // self.zl,
            ((z % self.zl) * self.ny + y) * 2 + core,
        )


def kernel(
    t, half, acts_hbm, key_hbm, value_hbm, out_ref,
    acts, sib_acts, cot_own, cot_give, cot_sib, first,
    py, pz, ry, rz, y1, z1, y1r, z1r, y2, z2, y2r, z2r, fin, fin_r,
    load_sem, pair_s, pair_r, ys, yr, zs, zr,
    y1s, y1v, z1s, z1v, y2s, y2v, z2s, z2v, fin_s, fin_v,
):
    nx, ny, nz, nzh, zl = t.nx, t.ny, t.nz, t.zh, t.zl
    x, y, z, core = t.here()
    my_zh = z // zl
    tokens, width = acts.shape
    per_x = width // nx
    block = per_x // nzh

    def wrap(v, n):
        return lax.rem(v + 2 * n, n)

    def at_x(d):
        return t.device(wrap(x + d, nx), y, z, core)

    def at_y(d):
        return t.device(x, wrap(y + d, ny), z, core)

    def at_z(d):
        return t.device(x, y, wrap(z + d, nz), core)

    sibling = t.device(x, y, z, 1 - core)

    def remote(src, dst, s, r, to):
        return pltpu.make_async_remote_copy(
            src, dst, s, r, device_id=to, device_id_type=MESH
        )

    barrier = pltpu.get_barrier_semaphore()
    peers = [sibling]
    peers += [at_x(d) for d in range(1, nx)]
    peers += [at_y(d) for d in range(1, ny)]
    peers += [at_z(d) for d in range(1, nz)]
    for peer in peers:
        pl.semaphore_signal(barrier, inc=1, device_id=peer, device_id_type=MESH)

    load_acts = pltpu.make_async_copy(acts_hbm, acts, load_sem.at[0])
    load_acts.start()

    @pl.when(core == 0)
    def _():
        pltpu.make_async_copy(key_hbm, cot_own, load_sem.at[1]).start()
        pltpu.make_async_copy(value_hbm, cot_give, load_sem.at[2]).start()

    @pl.when(core == 1)
    def _():
        pltpu.make_async_copy(value_hbm, cot_own, load_sem.at[1]).start()
        pltpu.make_async_copy(key_hbm, cot_give, load_sem.at[2]).start()

    pltpu.make_async_copy(key_hbm, cot_own, load_sem.at[1]).wait()
    pltpu.make_async_copy(key_hbm, cot_give, load_sem.at[2]).wait()
    load_acts.wait()
    pl.semaphore_wait(barrier, len(peers))

    give_cot = remote(cot_give, cot_sib, pair_s.at[0], pair_r.at[0], sibling)
    give_cot.start()
    order = [wrap(my_zh + d, nzh) for d in sorted(range(nzh), key=lambda d: -min(d, nzh - d))]

    def lanes(ix, izh):
        return pl.ds(pl.multiple_of(ix * per_x + izh * block, 128), block)

    pair = []
    for k in range(nzh):
        row = []
        for ix in range(nx):
            cut = lanes(ix, order[k])
            c = remote(
                acts.at[:, cut], sib_acts.at[:, cut],
                pair_s.at[1 + k * nx + ix], pair_r.at[1 + k * nx + ix], sibling,
            )
            c.start()
            row.append(c)
        pair.append(row)

    contract = (((0,), (0,)), ((), ()))

    def own_product(i, _):
        cut = pl.ds(pl.multiple_of(i * block, 128), block)
        first[pl.ds(pl.multiple_of(i * block, 128), block), :] = lax.dot_general(
            acts[:, cut], cot_own[...], contract, preferred_element_type=F32
        )
        return 0

    lax.fori_loop(0, nx * nzh, own_product, 0)
    give_cot.wait_recv()

    def chip_product(k):
        izh = order[k]

        def one(ix, _):
            cut = lanes(ix, izh)
            rows = first[pl.ds(pl.multiple_of(ix * per_x + izh * block, 128), block), :]
            rows += lax.dot_general(
                sib_acts[:, cut], cot_sib[...], contract, preferred_element_type=F32
            )
            rows = rows.astype(BF16).reshape(zl, ny, ROWS, 2 * half)
            for j in range(zl):
                py[:, ix, izh * zl + j] = rows[j, :, :, :half]
                pz[izh * zl + j, ix] = rows[j, :, :, half:]
            return 0

        for c in pair[k]:
            c.wait_recv()
        lax.fori_loop(0, nx, one, 0)

    started = []

    def hops(axis, n, p, piece, s, first_way):
        for way in (1, -1):
            count = n // 2 if way == first_way else n // 2 - 1
            if s > count:
                continue
            d = count - s + 1
            w = 0 if way == 1 else 1
            if axis == "y":
                mine = py.at[wrap(y + way * d, ny), :, pl.ds(piece * zl, zl)]
                slot = lambda q: ry.at[w, p, q - 1]
                ssem, rsem, to = ys, yr, at_y(way)
            else:
                mine = pz.at[wrap(z + way * d, nz), pl.ds(piece * (nx // 2), nx // 2)]
                slot = lambda q: rz.at[w, p, q - 1]
                ssem, rsem, to = zs, zr, at_z(way)
            if s > 1:
                before = remote(mine, slot(s - 1), ssem.at[w, p, s - 2], rsem.at[w, p, s - 2], to)
                before.wait_recv()
                mine[...] = (mine[...].astype(F32) + slot(s - 1)[...].astype(F32)).astype(BF16)
            c = remote(mine, slot(s), ssem.at[w, p, s - 1], rsem.at[w, p, s - 1], to)
            c.start()
            started.append(c)

    events = []
    for p in range(nzh):
        lead = 1 if p % 2 == 0 else -1
        for s in range(1, ny // 2 + 1):
            events.append(((s - 1 + 0.25 * p) / (ny // 2), "y", p, s, lead))
    for p in range(2):
        lead = 1 if p == 0 else -1
        for s in range(1, nz // 2 + 1):
            events.append(((s - 1 + 0.5 * p) / (nz // 2), "z", p, s, lead))
    events.sort(key=lambda e: e[0])

    def run(e):
        _, axis, p, s, lead = e
        if axis == "y":
            hops("y", ny, p, order[p], s, lead)
        else:
            hops("z", nz, p, p, s, lead)

    for k in range(nzh):
        chip_product(k)
    for e in events:
        run(e)

    def gather_y(p):
        piece = order[p]
        cut = pl.ds(piece * zl, zl)
        total = py[y, :, cut].astype(F32)
        for w in (0, 1):
            count = ny // 2 if (w == 0) == (p % 2 == 0) else ny // 2 - 1
            if count == 0:
                continue
            slot = ry.at[w, p, count - 1]
            remote(slot, slot, ys.at[w, p, count - 1], yr.at[w, p, count - 1], sibling).wait_recv()
            total += slot[...].astype(F32)
        y1[:, cut] = total.astype(BF16)

    def gather_z(p):
        cut = pl.ds(p * (nx // 2), nx // 2)
        total = pz[z, cut].astype(F32)
        for w in (0, 1):
            count = nz // 2 if (w == 0) == (p == 0) else nz // 2 - 1
            if count == 0:
                continue
            slot = rz.at[w, p, count - 1]
            remote(slot, slot, zs.at[w, p, count - 1], zr.at[w, p, count - 1], sibling).wait_recv()
            total += slot[...].astype(F32)
        z1[cut] = total.astype(BF16)

    def send_x(src, dst, ss, rs):
        for d in range(1, nx):
            c = remote(src.at[wrap(x + d, nx)], dst.at[d - 1], ss.at[d - 1], rs, at_x(d))
            c.start()
            started.append(c)

    for p in range(nzh):
        gather_y(p)
    send_x(y1, y1r, y1s, y1v)
    for p in range(2):
        gather_z(p)
    send_x(z1, z1r, z1s, z1v)

    def wait_all(buf, sem):
        remote(buf, buf, sem, sem, sibling).wait_recv()

    def fold(mine, received, n):
        total = mine.astype(F32)
        for i in range(n):
            total += received[i].astype(F32)
        return total

    wait_all(y1r, y1v)
    y2[...] = fold(y1[x], y1r, nx - 1).astype(BF16)
    for d in range(1, nz):
        c = remote(y2.at[wrap(z + d, nz)], y2r.at[d - 1], y2s.at[d - 1], y2v, at_z(d))
        c.start()
        started.append(c)
    wait_all(z1r, z1v)
    z2[...] = fold(z1[x], z1r, nx - 1).astype(BF16)
    for d in range(1, ny):
        c = remote(z2.at[wrap(y + d, ny)], z2r.at[d - 1], z2s.at[d - 1], z2v, at_y(d))
        c.start()
        started.append(c)
    wait_all(z2r, z2v)
    fin[:, half:] = fold(z2[y], z2r, ny - 1)
    wait_all(y2r, y2v)
    fin[:, :half] = fold(y2[z], y2r, nz - 1)

    keep = ROWS // 2
    swap = remote(fin.at[pl.ds((1 - core) * keep, keep)], fin_r, fin_s, fin_v, sibling)
    swap.start()
    wide = 2 * half
    out_ref[:, pl.ds(pl.multiple_of(core * wide, 128), wide)] = fin[pl.ds(core * keep, keep), :]
    swap.wait_recv()
    out_ref[:, pl.ds(pl.multiple_of((1 - core) * wide, 128), wide)] = fin_r[...]

    give_cot.wait_send()
    for row in pair:
        for c in row:
            c.wait_send()
    for c in started:
        c.wait_send()
    swap.wait_send()


def shards(t, acts, key_cot, value_cot):
    tokens, width = acts.shape
    cols = key_cot.shape[1]
    half = cols // 2
    nx, ny, nz, nzh, zl = t.nx, t.ny, t.nz, t.zh, t.zl
    dma = pltpu.SemaphoreType.DMA
    vmem = pltpu.VMEM
    hop_y, hop_z = ny // 2, nz // 2
    scratch = [
        vmem((tokens, width), BF16), vmem((tokens, width), BF16),
        vmem((tokens, cols), BF16), vmem((tokens, cols), BF16), vmem((tokens, cols), BF16),
        vmem((width, cols), F32),
        vmem((ny, nx, nz, ROWS, half), BF16), vmem((nz, nx, ny, ROWS, half), BF16),
        vmem((2, nzh, hop_y, nx, zl, ROWS, half), BF16),
        vmem((2, 2, hop_z, nx // 2, ny, ROWS, half), BF16),
        vmem((nx, nz, ROWS, half), BF16), vmem((nx, ny, ROWS, half), BF16),
        vmem((nx - 1, nz, ROWS, half), BF16), vmem((nx - 1, ny, ROWS, half), BF16),
        vmem((nz, ROWS, half), BF16), vmem((ny, ROWS, half), BF16),
        vmem((nz - 1, ROWS, half), BF16), vmem((ny - 1, ROWS, half), BF16),
        vmem((ROWS, cols), F32), vmem((ROWS // 2, cols), F32),
        dma((3,)), dma((1 + nzh * nx,)), dma((1 + nzh * nx,)),
        dma((2, nzh, hop_y)), dma((2, nzh, hop_y)), dma((2, 2, hop_z)), dma((2, 2, hop_z)),
        dma((nx - 1,)), dma(()), dma((nx - 1,)), dma(()),
        dma((nz - 1,)), dma(()), dma((ny - 1,)), dma(()),
        dma(()), dma(()),
    ]
    anywhere = pl.BlockSpec(memory_space=pl.ANY)
    return pl.pallas_call(
        functools.partial(kernel, t, half),
        out_shape=jax.ShapeDtypeStruct((ROWS // 2, 2 * cols), F32),
        in_specs=[anywhere] * 3,
        out_specs=pl.BlockSpec(memory_space=pltpu.VMEM),
        scratch_shapes=scratch,
        compiler_params=pltpu.CompilerParams(
            collective_id=0, has_side_effects=True, vmem_limit_bytes=56 * 2**20
        ),
        cost_estimate=pl.CostEstimate(
            flops=4 * tokens * width * cols, bytes_accessed=2 * tokens * (width + 2 * cols),
            transcendentals=0,
        ),
    )(acts, key_cot, value_cot)


def solution(mesh):
    t = Torus(mesh.shape["node"], mesh.shape["local"], 4, 8)
    placed = P(("node", "local"), None)
    return jax.shard_map(
        functools.partial(shards, t), mesh=mesh, in_specs=(placed,) * 3,
        out_specs=placed, check_vma=False,
    )
```

```python
import functools
import types

import jax
import jax.numpy as jnp
from jax import lax
from jax.experimental import pallas as pl
from jax.experimental.pallas import tpu as pltpu
from jax.sharding import PartitionSpec as P

MESH = pl.DeviceIdType.MESH
F32, BF16 = jnp.float32, jnp.bfloat16
ROWS = 16
TILE = 128


class Torus:
    def __init__(self, n_node, n_local, nx, ny):
        self.nx, self.ny = nx, ny
        self.zh = n_node // nx
        self.zl = n_local // (2 * ny)
        self.nz = self.zh * self.zl

    def here(self):
        node, local = lax.axis_index("node"), lax.axis_index("local")
        x, zh = node // self.zh, node % self.zh
        zl, yc = local // (2 * self.ny), local % (2 * self.ny)
        return x, yc // 2, zh * self.zl + zl, yc % 2

    def device(self, x, y, z, core):
        return (
            x * self.zh + z // self.zl,
            ((z % self.zl) * self.ny + y) * 2 + core,
        )


def buffers(t, tokens, width, cols):
    nx, ny, nz, nzh, zl = t.nx, t.ny, t.nz, t.zh, t.zl
    dma = pltpu.SemaphoreType.DMA
    block = width // (nx * nzh)
    n2, hx, hy, hz = nzh // 2, nx // 2, ny // 2, nz // 2

    def held(*shape, dtype=BF16):
        return pltpu.VMEM(shape, dtype)

    def slab(*shape, tiles=1):
        return pltpu.VMEM((*shape, ROWS, tiles * TILE), BF16)

    return dict(
        acts=held(nzh, tokens, nx * block), sib_acts=held(nzh, tokens, nx * block),
        cot_own=held(tokens, cols), cot_give=held(tokens, cols), cot_sib=held(tokens, cols),
        first=held(nzh, nx, block, cols, dtype=F32),
        px=slab(nx, nzh, zl, ny), py=slab(ny, nzh, nx, zl), pz=slab(nz, nx, ny, tiles=2),
        rx=slab(2, 2, hx, n2, zl, ny), ry=slab(2, 2, hy, n2, nx, zl), rz=slab(2, nx, hz, ny, tiles=2),
        x1=slab(ny, nzh, zl), x1r=slab(ny - 1, nzh, zl), y1=slab(nx, nzh, zl), y1r=slab(nx - 1, nzh, zl),
        xy2=slab(nzh, zl, tiles=2), xy2r=slab(nz - 1, tiles=2),
        z1=slab(nx, ny, tiles=2), z1r=slab(nx - 1, ny, tiles=2), z2=slab(ny, tiles=2), z2r=slab(ny - 1, tiles=2),
        fin=held(ROWS, cols, dtype=F32), fin_r=held(ROWS // 2, cols, dtype=F32),
        load_sem=dma((nzh * nx + 2,)), pair_s=dma((1 + nzh,)), pair_v=dma((1 + nzh,)),
        xs=dma((2, 2, hx)), xv=dma((2, 2, hx)), ys=dma((2, 2, hy)), yv=dma((2, 2, hy)),
        zs=dma((2, nx, hz)), zv=dma((2, nx, hz)),
        x1s=dma((ny - 1,)), x1v=dma(()), y1s=dma((nx - 1,)), y1v=dma(()), xy2s=dma((nzh, zl)), xy2v=dma(()),
        z1s=dma((nx - 1,)), z1v=dma(()), z2s=dma((ny - 1,)), z2v=dma(()),
        fin_s=dma(()), fin_v=dma(()),
    )


def kernel(t, names, acts_hbm, key_hbm, value_hbm, out_ref, *refs):
    b = types.SimpleNamespace(**dict(zip(names, refs)))
    nx, ny, nz, nzh, zl = t.nx, t.ny, t.nz, t.zh, t.zl
    x, y, z, core = t.here()
    my_zh, my_zl = z // zl, z % zl
    tokens, width = acts_hbm.shape
    cols = key_hbm.shape[1]
    per_x = width // nx
    block = per_x // nzh

    def wrap(v, n):
        return lax.rem(v + 2 * n, n)

    def at(axis, d):
        if axis == "x":
            return t.device(wrap(x + d, nx), y, z, core)
        if axis == "y":
            return t.device(x, wrap(y + d, ny), z, core)
        return t.device(x, y, wrap(z + d, nz), core)

    sibling = t.device(x, y, z, 1 - core)

    def remote(src, dst, s, v, to):
        return pltpu.make_async_remote_copy(src, dst, s, v, device_id=to, device_id_type=MESH)

    started = []

    def send(src, dst, s, v, to):
        c = remote(src, dst, s, v, to)
        c.start()
        started.append(c)

    def arrived(buf, v):
        remote(buf, buf, v, v, sibling).wait_recv()

    barrier = pltpu.get_barrier_semaphore()
    peers = [sibling]
    for axis, n in (("x", nx), ("y", ny), ("z", nz)):
        peers += [at(axis, d) for d in range(1, n)]
    for peer in peers:
        pl.semaphore_signal(barrier, inc=1, device_id=peer, device_id_type=MESH)

    n_load = nzh * nx

    @pl.when(core == 0)
    def _():
        pltpu.make_async_copy(key_hbm, b.cot_own, b.load_sem.at[n_load]).start()
        pltpu.make_async_copy(value_hbm, b.cot_give, b.load_sem.at[n_load + 1]).start()

    @pl.when(core == 1)
    def _():
        pltpu.make_async_copy(value_hbm, b.cot_own, b.load_sem.at[n_load]).start()
        pltpu.make_async_copy(key_hbm, b.cot_give, b.load_sem.at[n_load + 1]).start()

    away = sorted(range(nzh), key=lambda d: -min(d, nzh - d))
    order = [wrap(my_zh + d, nzh) for d in away]
    loads = []
    for k in range(nzh):
        for ix in range(nx):
            cut = pl.ds(pl.multiple_of(ix * per_x + order[k] * block, TILE), block)
            c = pltpu.make_async_copy(
                acts_hbm.at[:, cut], b.acts.at[k, :, pl.ds(ix * block, block)], b.load_sem.at[k * nx + ix]
            )
            c.start()
            loads.append(c)

    pltpu.make_async_copy(key_hbm, b.cot_own, b.load_sem.at[n_load]).wait()
    pltpu.make_async_copy(key_hbm, b.cot_give, b.load_sem.at[n_load + 1]).wait()
    pl.semaphore_wait(barrier, len(peers))

    send(b.cot_give, b.cot_sib, b.pair_s.at[0], b.pair_v.at[0], sibling)
    for k in range(nzh):
        for c in loads[k * nx : (k + 1) * nx]:
            c.wait()
        send(b.acts.at[k], b.sib_acts.at[k], b.pair_s.at[1 + k], b.pair_v.at[1 + k], sibling)

    def dot(acts, k, ix, cot):
        cut = pl.ds(pl.multiple_of(ix * block, TILE), block)
        return lax.dot_general(
            acts[k, :, cut], cot[...], (((0,), (0,)), ((), ())), preferred_element_type=F32
        )

    def own_product(k):
        def one(ix, _):
            b.first[k, ix] = dot(b.acts, k, ix, b.cot_own)
            return 0

        lax.fori_loop(0, nx, one, 0)

    def chip_product(k):
        izh = order[k]

        def one(ix, _):
            rows = b.first[k, ix] + dot(b.sib_acts, k, ix, b.cot_sib)
            rows = rows.astype(BF16).reshape(zl, ny, ROWS, cols)
            b.px[ix, k] = rows[..., :TILE]
            for j in range(zl):
                b.py[:, k, ix, j] = rows[j, :, :, TILE : 2 * TILE]
            b.pz[pl.ds(izh * zl, zl), ix] = rows[..., 2 * TILE :]
            return 0

        if k == 0:
            arrived(b.cot_sib, b.pair_v.at[0])
        arrived(b.sib_acts.at[k], b.pair_v.at[1 + k])
        lax.fori_loop(0, nx, one, 0)

    n2 = nzh // 2

    def ring(axis, p):
        if axis == "x":
            return (
                nx, x, lambda to: b.px.at[to, pl.ds(p * n2, n2)], lambda w, q: b.rx.at[w, p, q],
                lambda w, q: (b.xs.at[w, p, q], b.xv.at[w, p, q]), p,
            )
        if axis == "y":
            return (
                ny, y, lambda to: b.py.at[to, pl.ds(p * n2, n2)], lambda w, q: b.ry.at[w, p, q],
                lambda w, q: (b.ys.at[w, p, q], b.yv.at[w, p, q]), p,
            )
        return (
            nz, z, lambda to: b.pz.at[to, p], lambda w, q: b.rz.at[w, p, q],
            lambda w, q: (b.zs.at[w, p, q], b.zv.at[w, p, q]), 0 if p < nx // 2 else 1,
        )

    def count(n, w, long_way):
        return n // 2 if w == long_way else n // 2 - 1

    def hop(axis, p, w, s):
        n, me, sums, slot, sems, long_way = ring(axis, p)
        hops, way = count(n, w, long_way), 1 - 2 * w
        if s > hops:
            return
        mine = sums(wrap(me + way * (hops - s + 1), n))
        if s > 1:
            arrived(slot(w, s - 2), sems(w, s - 2)[1])
            mine[...] = (mine[...].astype(F32) + slot(w, s - 2)[...].astype(F32)).astype(BF16)
        send(mine, slot(w, s - 1), *sems(w, s - 1), at(axis, way))

    def gathered(axis, p):
        n, me, sums, slot, sems, long_way = ring(axis, p)
        total = sums(me)[...].astype(F32)
        for w in (0, 1):
            hops = count(n, w, long_way)
            if hops > 0:
                arrived(slot(w, hops - 1), sems(w, hops - 1)[1])
                total += slot(w, hops - 1)[...].astype(F32)
        return total.astype(BF16)

    def fold(mine, received, n):
        total = mine.astype(F32)
        for i in range(n):
            total += received[i].astype(F32)
        return total

    def to_line(axis, n, me, src, dst, ss, v):
        for d in range(1, n):
            send(src.at[wrap(me + d, n)], dst.at[d - 1], ss.at[d - 1], v, at(axis, d))

    def gather_x():
        for p in (0, 1):
            rows = gathered("x", p)
            for g in range(n2):
                for j in range(zl):
                    b.x1[:, p * n2 + g, j] = rows[g, j]
        to_line("y", ny, y, b.x1, b.x1r, b.x1s, b.x1v)

    def gather_y():
        for p in (1, 0):
            rows = gathered("y", p)
            for g in range(n2):
                b.y1[:, p * n2 + g] = rows[g]
        to_line("x", nx, x, b.y1, b.y1r, b.y1s, b.y1v)

    def fold_x():
        arrived(b.x1r, b.x1v)
        b.xy2[:, :, :, :TILE] = fold(b.x1[y], b.x1r, ny - 1).astype(BF16)

    def fold_y():
        arrived(b.y1r, b.y1v)
        b.xy2[:, :, :, TILE:] = fold(b.y1[x], b.y1r, nx - 1).astype(BF16)
        for k in range(nzh):
            own = away[k] == 0
            for j in range(zl - 1 if own else zl):
                row = lax.rem(my_zl + 1 + j, zl) if own else j
                to = order[k] * zl + row
                send(
                    b.xy2.at[k, row], b.xy2r.at[wrap(to - z, nz) - 1], b.xy2s.at[k, j], b.xy2v,
                    t.device(x, y, to, core),
                )

    def gather_z():
        for p in [*range(nx // 2, nx), *range(nx // 2)]:
            b.z1[p] = gathered("z", p)
        to_line("x", nx, x, b.z1, b.z1r, b.z1s, b.z1v)

    def fold_z():
        arrived(b.z1r, b.z1v)
        b.z2[...] = fold(b.z1[x], b.z1r, nx - 1).astype(BF16)
        to_line("y", ny, y, b.z2, b.z2r, b.z2s, b.z2v)

    def drain():
        for c in started:
            c.wait_send()
        started.clear()

    def end_xy():
        arrived(b.xy2r, b.xy2v)
        b.fin[:, : 2 * TILE] = fold(b.xy2[nzh - 1, my_zl], b.xy2r, nz - 1)

    def end_z():
        arrived(b.z2r, b.z2v)
        b.fin[:, 2 * TILE :] = fold(b.z2[y], b.z2r, ny - 1)

    events = []

    def add(time, f, *args):
        events.append((time, functools.partial(f, *args)))

    ready = [2.5 + 1.5 * k for k in range(nzh)]
    for k in range(nzh):
        add(1.5 * k, own_product, k)
        add(ready[k], chip_product, k)
    most = ready[max(nzh - 2, 0)]
    for w in (0, 1):
        for p in (0, 1):
            half = ready[n2 - 1 if p == 0 else nzh - 1] + 0.1
            for s in range(1, nx // 2 + 1):
                add(half + 7.5 * (s - 1) + 0.1, hop, "x", p, w, s)
            for s in range(1, ny // 2 + 1):
                add(half + 5.1 * (s - 1), hop, "y", p, w, s)
        for p in range(nx):
            first = ready[0] + 0.1 if w == (0 if p < nx // 2 else 1) else most + 0.2
            for s in range(1, nz // 2 + 1):
                add(first + 5.1 * (s - 1) + 0.01 * p, hop, "z", p, w, s)
    add(22.0, gather_x)
    add(25.0, gather_y)
    add(27.5, fold_x)
    add(30.0, fold_y)
    add(33.4, gather_z)
    add(37.5, fold_z)
    add(38.0, drain)
    add(40.0, end_xy)
    add(42.0, end_z)
    for _, step in sorted(events, key=lambda e: e[0]):
        step()

    keep = ROWS // 2
    send(b.fin.at[pl.ds((1 - core) * keep, keep)], b.fin_r, b.fin_s, b.fin_v, sibling)
    out_ref[:, pl.ds(pl.multiple_of(core * cols, TILE), cols)] = b.fin[pl.ds(core * keep, keep), :]
    arrived(b.fin_r, b.fin_v)
    out_ref[:, pl.ds(pl.multiple_of((1 - core) * cols, TILE), cols)] = b.fin_r[...]
    drain()


def shards(t, acts, key_cot, value_cot):
    tokens, width = acts.shape
    cols = key_cot.shape[1]
    held = buffers(t, tokens, width, cols)
    anywhere = pl.BlockSpec(memory_space=pl.ANY)
    return pl.pallas_call(
        functools.partial(kernel, t, tuple(held)),
        out_shape=jax.ShapeDtypeStruct((ROWS // 2, 2 * cols), F32),
        in_specs=[anywhere] * 3,
        out_specs=pl.BlockSpec(memory_space=pltpu.VMEM),
        scratch_shapes=list(held.values()),
        compiler_params=pltpu.CompilerParams(
            collective_id=0, has_side_effects=True, vmem_limit_bytes=56 * 2**20
        ),
        cost_estimate=pl.CostEstimate(
            flops=4 * tokens * width * cols, bytes_accessed=2 * tokens * (width + 2 * cols),
            transcendentals=0,
        ),
    )(acts, key_cot, value_cot)


def solution(mesh):
    t = Torus(mesh.shape["node"], mesh.shape["local"], 4, 8)
    placed = P(("node", "local"), None)
    return jax.shard_map(
        functools.partial(shards, t), mesh=mesh, in_specs=(placed,) * 3,
        out_specs=placed, check_vma=False,
    )
```

```python
import functools
import types

import jax
import jax.numpy as jnp
from jax import lax
from jax.experimental import pallas as pl
from jax.experimental.pallas import tpu as pltpu
from jax.sharding import PartitionSpec as P

MESH = pl.DeviceIdType.MESH
F32, BF16 = jnp.float32, jnp.bfloat16
ROWS = 16
TILE = 128


class Torus:
    def __init__(self, n_node, n_local, nx, ny):
        self.nx, self.ny = nx, ny
        self.zh = n_node // nx
        self.zl = n_local // (2 * ny)
        self.nz = self.zh * self.zl

    def here(self):
        node, local = lax.axis_index("node"), lax.axis_index("local")
        x, zh = node // self.zh, node % self.zh
        zl, yc = local // (2 * self.ny), local % (2 * self.ny)
        return x, yc // 2, zh * self.zl + zl, yc % 2

    def device(self, x, y, z, core):
        return (
            x * self.zh + z // self.zl,
            ((z % self.zl) * self.ny + y) * 2 + core,
        )


def buffers(t, tokens, width, cols):
    nx, ny, nz = t.nx, t.ny, t.nz
    dma = pltpu.SemaphoreType.DMA
    n2, hx, hy, hz = nz // 2, nx // 2, ny // 2, nz // 2

    def held(*shape, dtype=BF16):
        return pltpu.VMEM(shape, dtype)

    def slab(*shape, tiles=1):
        return pltpu.VMEM((*shape, ROWS, tiles * TILE), BF16)

    return dict(
        acts=held(nx, tokens, width // nx), sib_acts=held(nx, tokens, width // nx),
        cot_own=held(tokens, cols), cot_give=held(tokens, cols), cot_sib=held(tokens, cols),
        first=held(nz, width // nz, cols, dtype=F32),
        px=slab(nx, nz, ny), py=slab(ny, nz, nx), pz=slab(nz, nx, ny, tiles=2),
        rx=slab(2, 2, hx, n2, ny), ry=slab(2, 2, hy, n2, nx), rz=slab(2, nx, hz, ny, tiles=2),
        x1=slab(2, ny, n2), x1r=slab(2, ny - 1, n2), y1=slab(nx, nz), y1r=slab(nx - 1, nz),
        xy2=slab(nz, tiles=2), xy2r=slab(nz - 1, tiles=2),
        z1=slab(nx, ny, tiles=2), z1r=slab(nx - 1, ny, tiles=2), z2=slab(ny, tiles=2), z2r=slab(ny - 1, tiles=2),
        fin=held(ROWS, cols, dtype=F32), fin_r=held(ROWS // 2, cols, dtype=F32),
        load_sem=dma((nx + 2,)), pair_s=dma((1 + nz,)), pair_v=dma((1 + nz,)),
        xs=dma((2, 2, hx)), xv=dma((2, 2, hx)), ys=dma((2, 2, hy)), yv=dma((2, 2, hy)),
        zs=dma((2, nx, hz)), zv=dma((2, nx, hz)),
        x1s=dma((2, ny - 1)), x1v=dma((2,)), y1s=dma((nx - 1,)), y1v=dma(()), xy2s=dma((nz - 1,)), xy2v=dma(()),
        z1s=dma((nx - 1,)), z1v=dma(()), z2s=dma((ny - 1,)), z2v=dma(()),
        fin_s=dma(()), fin_v=dma(()),
    )


def kernel(t, names, acts_hbm, key_hbm, value_hbm, out_ref, *refs):
    b = types.SimpleNamespace(**dict(zip(names, refs)))
    nx, ny, nz = t.nx, t.ny, t.nz
    x, y, z, core = t.here()
    tokens, width = acts_hbm.shape
    cols = key_hbm.shape[1]
    per_x = width // nx
    block = per_x // nz

    def wrap(v, n):
        return lax.rem(v + 2 * n, n)

    @functools.cache
    def at(axis, d):
        if axis == "x":
            return t.device(wrap(x + d, nx), y, z, core)
        if axis == "y":
            return t.device(x, wrap(y + d, ny), z, core)
        return t.device(x, y, wrap(z + d, nz), core)

    sibling = t.device(x, y, z, 1 - core)

    def remote(src, dst, s, v, to):
        return pltpu.make_async_remote_copy(src, dst, s, v, device_id=to, device_id_type=MESH)

    started = []

    def send(src, dst, s, v, to):
        c = remote(src, dst, s, v, to)
        c.start()
        started.append(c)

    def arrived(buf, v):
        remote(buf, buf, v, v, sibling).wait_recv()

    barrier = pltpu.get_barrier_semaphore()
    peers = [sibling]
    for axis, n in (("x", nx), ("y", ny), ("z", nz)):
        peers += [at(axis, d) for d in range(1, n)]
    for peer in peers:
        pl.semaphore_signal(barrier, inc=1, device_id=peer, device_id_type=MESH)

    n_load = nx

    @pl.when(core == 0)
    def _():
        pltpu.make_async_copy(key_hbm, b.cot_own, b.load_sem.at[n_load]).start()
        pltpu.make_async_copy(value_hbm, b.cot_give, b.load_sem.at[n_load + 1]).start()

    @pl.when(core == 1)
    def _():
        pltpu.make_async_copy(value_hbm, b.cot_own, b.load_sem.at[n_load]).start()
        pltpu.make_async_copy(key_hbm, b.cot_give, b.load_sem.at[n_load + 1]).start()

    loads = []
    for ix in range(nx):
        c = pltpu.make_async_copy(
            acts_hbm.at[:, pl.ds(ix * per_x, per_x)], b.acts.at[ix], b.load_sem.at[ix]
        )
        c.start()
        loads.append(c)

    pltpu.make_async_copy(key_hbm, b.cot_own, b.load_sem.at[n_load]).wait()
    pltpu.make_async_copy(key_hbm, b.cot_give, b.load_sem.at[n_load + 1]).wait()
    for c in loads:
        c.wait()
    pl.semaphore_wait(barrier, len(peers))

    offs = [nz // 2]
    for d in range(nz // 2 - 1, 0, -1):
        offs += [d, -d]
    offs.append(0)

    def cut(i):
        return pl.ds(pl.multiple_of(wrap(z + offs[i], nz) * block, TILE), block)

    send(b.cot_give, b.cot_sib, b.pair_s.at[0], b.pair_v.at[0], sibling)
    for i in range(nz):
        part = (slice(None), slice(None), cut(i))
        send(b.acts.at[part], b.sib_acts.at[part], b.pair_s.at[1 + i], b.pair_v.at[1 + i], sibling)

    def dot(acts, i, cot):
        rows = jnp.concatenate([acts[ix, :, cut(i)] for ix in range(nx)], axis=1)
        return lax.dot_general(
            rows, cot[...], (((0,), (0,)), ((), ())), preferred_element_type=F32
        )

    def own_product(i):
        b.first[i] = dot(b.acts, i, b.cot_own)

    def chip_product(i):
        if i == 0:
            arrived(b.cot_sib, b.pair_v.at[0])
        arrived(b.sib_acts.at[:, :, cut(i)], b.pair_v.at[1 + i])
        rows = b.first[i] + dot(b.sib_acts, i, b.cot_sib)
        rows = rows.astype(BF16).reshape(nx, ny, ROWS, cols)
        b.px[:, i] = rows[..., :TILE]
        for ix in range(nx):
            b.py[:, i, ix] = rows[ix, :, :, TILE : 2 * TILE]
        b.pz[i] = rows[..., 2 * TILE :]

    n2 = nz // 2

    def ring(axis, p):
        half = pl.ds(p * n2, n2)
        if axis == "x":
            return (
                nx, lambda d: b.px.at[wrap(x + d, nx), half], lambda w, q: b.rx.at[w, p, q],
                lambda w, q: (b.xs.at[w, p, q], b.xv.at[w, p, q]), p,
            )
        if axis == "y":
            return (
                ny, lambda d: b.py.at[wrap(y + d, ny), half], lambda w, q: b.ry.at[w, p, q],
                lambda w, q: (b.ys.at[w, p, q], b.yv.at[w, p, q]), p,
            )
        return (
            nz, lambda d: b.pz.at[offs.index(n2 if d == -n2 else d), p], lambda w, q: b.rz.at[w, p, q],
            lambda w, q: (b.zs.at[w, p, q], b.zv.at[w, p, q]), 0 if p < nx // 2 else 1,
        )

    def count(n, w, long_way):
        return n // 2 if w == long_way else n // 2 - 1

    def hop(axis, p, w, s):
        n, sums, slot, sems, long_way = ring(axis, p)
        hops, way = count(n, w, long_way), 1 - 2 * w
        if s > hops:
            return
        mine = sums(way * (hops - s + 1))
        if s > 1:
            arrived(slot(w, s - 2), sems(w, s - 2)[1])
            mine[...] = (mine[...].astype(F32) + slot(w, s - 2)[...].astype(F32)).astype(BF16)
        send(mine, slot(w, s - 1), *sems(w, s - 1), at(axis, way))

    def gathered(axis, p):
        n, sums, slot, sems, long_way = ring(axis, p)
        total = sums(0)[...].astype(F32)
        for w in (0, 1):
            hops = count(n, w, long_way)
            if hops > 0:
                arrived(slot(w, hops - 1), sems(w, hops - 1)[1])
                total += slot(w, hops - 1)[...].astype(F32)
        return total.astype(BF16)

    def fold(mine, received, n):
        total = mine.astype(F32)
        for i in range(n):
            total += received[i].astype(F32)
        return total

    def to_line(axis, n, me, src, dst, ss, v):
        for d in range(1, n):
            send(src.at[wrap(me + d, n)], dst.at[d - 1], ss.at[d - 1], v, at(axis, d))

    def gather_x(p):
        rows = gathered("x", p)
        for g in range(n2):
            b.x1[p, :, g] = rows[g]
        to_line("y", ny, y, b.x1.at[p], b.x1r.at[p], b.x1s.at[p], b.x1v.at[p])

    def gather_y():
        for p in (1, 0):
            rows = gathered("y", p)
            for g in range(n2):
                b.y1[:, p * n2 + g] = rows[g]
        to_line("x", nx, x, b.y1, b.y1r, b.y1s, b.y1v)

    def fold_x(p):
        arrived(b.x1r.at[p], b.x1v.at[p])
        b.xy2[p * n2 : (p + 1) * n2, :, :TILE] = fold(b.x1[p, y], b.x1r.at[p], ny - 1).astype(BF16)

    def fold_y():
        arrived(b.y1r, b.y1v)
        b.xy2[:, :, TILE:] = fold(b.y1[x], b.y1r, nx - 1).astype(BF16)
        for i in range(nz - 1):
            send(b.xy2.at[i], b.xy2r.at[offs[i] % nz - 1], b.xy2s.at[i], b.xy2v, at("z", offs[i] % nz))

    def gather_z():
        for p in [*range(nx // 2, nx), *range(nx // 2)]:
            b.z1[p] = gathered("z", p)
        to_line("x", nx, x, b.z1, b.z1r, b.z1s, b.z1v)

    def fold_z():
        arrived(b.z1r, b.z1v)
        b.z2[...] = fold(b.z1[x], b.z1r, nx - 1).astype(BF16)
        to_line("y", ny, y, b.z2, b.z2r, b.z2s, b.z2v)

    def drain():
        for c in started:
            c.wait_send()
        started.clear()

    def end_xy():
        arrived(b.xy2r, b.xy2v)
        b.fin[:, : 2 * TILE] = fold(b.xy2[nz - 1], b.xy2r, nz - 1)

    def end_z():
        arrived(b.z2r, b.z2v)
        b.fin[:, 2 * TILE :] = fold(b.z2[y], b.z2r, ny - 1)

    events = []

    def add(time, f, *args):
        events.append((time, functools.partial(f, *args)))

    ready = [2.2 + 0.5 * i for i in range(nz)]
    for i in range(nz):
        add(0.0 if i < 2 else ready[i - 2] + 0.2, own_product, i)
        add(ready[i], chip_product, i)
    for w in (0, 1):
        for p in (0, 1):
            half = ready[(p + 1) * n2 - 1] + 0.1
            for s in range(1, nx // 2 + 1):
                add(half + 7.2 * (s - 1) + 0.1, hop, "x", p, w, s)
            for s in range(1, ny // 2 + 1):
                add(half + 5.1 * (s - 1), hop, "y", p, w, s)
        for p in range(nx):
            begin = ready[0] + 0.1 if w == (0 if p < nx // 2 else 1) else ready[min(2, nz - 1)] + 0.1
            for s in range(1, nz // 2 + 1):
                add(begin + (5.1 if begin < ready[0] + 0.2 else 5.5) * (s - 1) + 0.01 * p, hop, "z", p, w, s)
    add(19.0, gather_x, 0)
    add(22.5, gather_x, 1)
    add(26.0, gather_y)
    add(31.0, fold_x, 0)
    add(31.1, fold_x, 1)
    add(31.2, fold_y)
    add(33.0, gather_z)
    add(33.1, drain)
    add(37.0, fold_z)
    add(40.0, end_xy)
    add(42.0, end_z)
    for _, step in sorted(events, key=lambda e: e[0]):
        step()

    keep = ROWS // 2
    send(b.fin.at[pl.ds((1 - core) * keep, keep)], b.fin_r, b.fin_s, b.fin_v, sibling)
    out_ref[:, pl.ds(pl.multiple_of(core * cols, TILE), cols)] = b.fin[pl.ds(core * keep, keep), :]
    arrived(b.fin_r, b.fin_v)
    out_ref[:, pl.ds(pl.multiple_of((1 - core) * cols, TILE), cols)] = b.fin_r[...]
    drain()


def shards(t, acts, key_cot, value_cot):
    tokens, width = acts.shape
    cols = key_cot.shape[1]
    held = buffers(t, tokens, width, cols)
    anywhere = pl.BlockSpec(memory_space=pl.ANY)
    return pl.pallas_call(
        functools.partial(kernel, t, tuple(held)),
        out_shape=jax.ShapeDtypeStruct((ROWS // 2, 2 * cols), F32),
        in_specs=[anywhere] * 3,
        out_specs=pl.BlockSpec(memory_space=pltpu.VMEM),
        scratch_shapes=list(held.values()),
        compiler_params=pltpu.CompilerParams(
            collective_id=0, has_side_effects=True, vmem_limit_bytes=56 * 2**20
        ),
        cost_estimate=pl.CostEstimate(
            flops=4 * tokens * width * cols, bytes_accessed=2 * tokens * (width + 2 * cols),
            transcendentals=0,
        ),
    )(acts, key_cot, value_cot)


def solution(mesh):
    t = Torus(mesh.shape["node"], mesh.shape["local"], 4, 8)
    placed = P(("node", "local"), None)
    return jax.shard_map(
        functools.partial(shards, t), mesh=mesh, in_specs=(placed,) * 3,
        out_specs=placed, check_vma=False,
    )
```

```python
import functools
import types

import jax
import jax.numpy as jnp
from jax import lax
from jax.experimental import pallas as pl
from jax.experimental.pallas import tpu as pltpu
from jax.sharding import PartitionSpec as P

MESH = pl.DeviceIdType.MESH
F32, BF16 = jnp.float32, jnp.bfloat16
ROWS = 16
TILE = 128


class Torus:
    def __init__(self, n_node, n_local, nx, ny):
        self.nx, self.ny = nx, ny
        self.zh = n_node // nx
        self.zl = n_local // (2 * ny)
        self.nz = self.zh * self.zl

    def here(self):
        node, local = lax.axis_index("node"), lax.axis_index("local")
        x, zh = node // self.zh, node % self.zh
        zl, yc = local // (2 * self.ny), local % (2 * self.ny)
        return x, yc // 2, zh * self.zl + zl, yc % 2

    def device(self, x, y, z, core):
        return (
            x * self.zh + z // self.zl,
            ((z % self.zl) * self.ny + y) * 2 + core,
        )


def shared_buffers(t, tokens, width, cols):
    nx, nz = t.nx, t.nz
    dma = pltpu.SemaphoreType.DMA

    def held(*shape, dtype=BF16):
        return pltpu.VMEM(shape, dtype)

    return dict(
        acts=held(nx, tokens, width // nx), sib_acts=held(nx, tokens, width // nx),
        cot_own=held(tokens, cols), cot_give=held(tokens, cols), cot_sib=held(tokens, cols),
        first=held(nz, width // nz, cols, dtype=F32),
        fin=held(ROWS, cols, dtype=F32), fin_r=held(ROWS // 2, cols, dtype=F32),
        load_sem=dma((nx + 2,)), pair_s=dma((1 + nz,)), pair_v=dma((1 + nz,)),
        fin_s=dma(()), fin_v=dma(()),
    )


def core_buffers(t, xt, zt):
    nx, ny, nz = t.nx, t.ny, t.nz
    dma = pltpu.SemaphoreType.DMA
    n2, hx, hy, hz = nz // 2, nx // 2, ny // 2, nz // 2

    def slab(*shape, tiles=1):
        return pltpu.VMEM((*shape, ROWS, tiles * TILE), BF16)

    return dict(
        px=slab(nx, nz, ny, tiles=xt), py=slab(ny, nz, nx), pz=slab(nz, nx, ny, tiles=zt),
        rx=slab(2, 2, hx, n2, ny, tiles=xt), ry=slab(2, 2, hy, n2, nx), rz=slab(2, nx, hz, ny, tiles=zt),
        x1=slab(ny, n2, tiles=xt), x1r=slab(ny - 1, n2, tiles=xt),
        xn=slab(n2, ny, tiles=xt), xnr=slab(max(n2 - 1, 1), ny, tiles=xt),
        y1=slab(nx, nz), y1r=slab(nx - 1, nz),
        far=slab(n2, tiles=xt + 1), far_r=slab(n2, tiles=xt + 1), near=slab(n2), near_r=slab(max(n2 - 1, 1)),
        z1=slab(nx, ny, tiles=zt), z1r=slab(nx - 1, ny, tiles=zt), z2=slab(ny, tiles=zt + xt), z2r=slab(ny - 1, tiles=zt + xt),
        xs=dma((2, 2, hx)), xv=dma((2, 2, hx)), ys=dma((2, 2, hy)), yv=dma((2, 2, hy)),
        zs=dma((2, nx, hz)), zv=dma((2, nx, hz)),
        x1s=dma((ny - 1,)), x1v=dma(()), y1s=dma((nx - 1,)), y1v=dma(()), xns=dma((n2,)), xnv=dma(()),
        far_s=dma((n2,)), far_v=dma(()), near_s=dma((n2,)), near_v=dma(()),
        z1s=dma((nx - 1,)), z1v=dma(()), z2s=dma((ny - 1,)), z2v=dma(()),
    )


SHARES = ((2, 1), (1, 2))


def kernel(t, names, acts_hbm, key_hbm, value_hbm, out_ref, *refs):
    held = dict(zip(names, refs))
    b = types.SimpleNamespace(**{n: r for (c, n), r in held.items() if c is None})
    nx, ny, nz = t.nx, t.ny, t.nz
    x, y, z, core = t.here()
    tokens, width = acts_hbm.shape
    cols = key_hbm.shape[1]
    per_x = width // nx
    block = per_x // nz

    def wrap(v, n):
        return lax.rem(v + 2 * n, n)

    line = {("x", d): t.device(wrap(x + d, nx), y, z, core) for d in range(1, nx)}
    line.update({("y", d): t.device(x, wrap(y + d, ny), z, core) for d in range(1, ny)})
    line.update({("z", d): t.device(x, y, wrap(z + d, nz), core) for d in range(1, nz)})
    size = {"x": nx, "y": ny, "z": nz}

    def at(axis, d):
        return line[axis, d % size[axis]]

    sibling = t.device(x, y, z, 1 - core)

    def remote(src, dst, s, v, to):
        return pltpu.make_async_remote_copy(src, dst, s, v, device_id=to, device_id_type=MESH)

    started = []

    def send(src, dst, s, v, to):
        c = remote(src, dst, s, v, to)
        c.start()
        started.append(c)

    def arrived(buf, v):
        remote(buf, buf, v, v, sibling).wait_recv()

    barrier = pltpu.get_barrier_semaphore()
    peers = [sibling] + [line[a, d] for a, n in size.items() for d in sorted({1, n - 1})]
    for peer in peers:
        pl.semaphore_signal(barrier, inc=1, device_id=peer, device_id_type=MESH)

    n_load = nx

    @pl.when(core == 0)
    def _():
        pltpu.make_async_copy(key_hbm, b.cot_own, b.load_sem.at[n_load]).start()
        pltpu.make_async_copy(value_hbm, b.cot_give, b.load_sem.at[n_load + 1]).start()

    @pl.when(core == 1)
    def _():
        pltpu.make_async_copy(value_hbm, b.cot_own, b.load_sem.at[n_load]).start()
        pltpu.make_async_copy(key_hbm, b.cot_give, b.load_sem.at[n_load + 1]).start()

    loads = []
    for ix in range(nx):
        c = pltpu.make_async_copy(
            acts_hbm.at[:, pl.ds(ix * per_x, per_x)], b.acts.at[ix], b.load_sem.at[ix]
        )
        c.start()
        loads.append(c)

    pltpu.make_async_copy(key_hbm, b.cot_own, b.load_sem.at[n_load]).wait()
    pltpu.make_async_copy(key_hbm, b.cot_give, b.load_sem.at[n_load + 1]).wait()
    for c in loads:
        c.wait()
    pl.semaphore_wait(barrier, len(peers))

    offs = [nz // 2]
    for d in range(nz // 2 - 1, 0, -1):
        offs += [d, -d]
    offs.append(0)

    def cut(i):
        return pl.ds(pl.multiple_of(wrap(z + offs[i], nz) * block, TILE), block)

    send(b.cot_give, b.cot_sib, b.pair_s.at[0], b.pair_v.at[0], sibling)
    for i in range(nz):
        part = (slice(None), slice(None), cut(i))
        send(b.acts.at[part], b.sib_acts.at[part], b.pair_s.at[1 + i], b.pair_v.at[1 + i], sibling)

    def work(c):
        mine = list(started)

        def send(*args):
            copy = remote(*args)
            copy.start()
            mine.append(copy)

        b = types.SimpleNamespace(**{n: r for (of, n), r in held.items() if of in (None, c)})
        to_y = SHARES[c][0] * TILE
        to_z = to_y + TILE

        def dot(acts, i, cot):
            rows = jnp.concatenate([acts[ix, :, cut(i)] for ix in range(nx)], axis=1)
            return lax.dot_general(
                rows, cot[...], (((0,), (0,)), ((), ())), preferred_element_type=F32
            )

        def own_product(i):
            b.first[i] = dot(b.acts, i, b.cot_own)

        def chip_product(i):
            if i == 0:
                arrived(b.cot_sib, b.pair_v.at[0])
            arrived(b.sib_acts.at[:, :, cut(i)], b.pair_v.at[1 + i])
            rows = b.first[i] + dot(b.sib_acts, i, b.cot_sib)
            rows = rows.astype(BF16).reshape(nx, ny, ROWS, cols)
            b.px[:, i] = rows[..., :to_y]
            for ix in range(nx):
                b.py[:, i, ix] = rows[ix, :, :, to_y:to_z]
            b.pz[i] = rows[..., to_z:]

        n2 = nz // 2

        def ring(axis, p):
            half = pl.ds(p * n2, n2)
            if axis == "x":
                return (
                    nx, lambda d: b.px.at[wrap(x + d, nx), half], lambda w, q: b.rx.at[w, p, q],
                    lambda w, q: (b.xs.at[w, p, q], b.xv.at[w, p, q]), p,
                )
            if axis == "y":
                return (
                    ny, lambda d: b.py.at[wrap(y + d, ny), half], lambda w, q: b.ry.at[w, p, q],
                    lambda w, q: (b.ys.at[w, p, q], b.yv.at[w, p, q]), p,
                )
            return (
                nz, lambda d: b.pz.at[offs.index(n2 if d == -n2 else d), p], lambda w, q: b.rz.at[w, p, q],
                lambda w, q: (b.zs.at[w, p, q], b.zv.at[w, p, q]), 0 if p < nx // 2 else 1,
            )

        def count(n, w, long_way):
            return n // 2 if w == long_way else n // 2 - 1

        def hop(axis, p, w, s):
            n, sums, slot, sems, long_way = ring(axis, p)
            hops, way = count(n, w, long_way), 1 - 2 * w
            if s > hops:
                return
            chunk = sums(way * (hops - s + 1))
            if s > 1:
                arrived(slot(w, s - 2), sems(w, s - 2)[1])
                chunk[...] = (chunk[...].astype(F32) + slot(w, s - 2)[...].astype(F32)).astype(BF16)
            send(chunk, slot(w, s - 1), *sems(w, s - 1), at(axis, way))

        def gathered(axis, p):
            n, sums, slot, sems, long_way = ring(axis, p)
            total = sums(0)[...].astype(F32)
            for w in (0, 1):
                hops = count(n, w, long_way)
                if hops > 0:
                    arrived(slot(w, hops - 1), sems(w, hops - 1)[1])
                    total += slot(w, hops - 1)[...].astype(F32)
            return total.astype(BF16)

        def fold(mine, received, n):
            total = mine.astype(F32)
            for i in range(n):
                total += received[i].astype(F32)
            return total

        def to_line(axis, n, me, src, dst, ss, v):
            for d in range(1, n):
                send(src.at[wrap(me + d, n)], dst.at[d - 1], ss.at[d - 1], v, at(axis, d))

        def gather_xy():
            rows = gathered("x", 0)
            for g in range(n2):
                b.x1[:, g] = rows[g]
            for p in (1, 0):
                rows = gathered("y", p)
                for g in range(n2):
                    b.y1[:, p * n2 + g] = rows[g]
            to_line("y", ny, y, b.x1, b.x1r, b.x1s, b.x1v)
            to_line("x", nx, x, b.y1, b.y1r, b.y1s, b.y1v)

        def gather_z():
            for p in [*range(nx // 2, nx), *range(nx // 2)]:
                b.z1[p] = gathered("z", p)
            to_line("x", nx, x, b.z1, b.z1r, b.z1s, b.z1v)

        def to_places(places, src, dst, ss, v):
            for g, d in enumerate(places):
                send(src.at[g], dst.at[g], ss.at[g], v, at("z", d))

        def gather_near():
            b.xn[...] = gathered("x", 1)
            to_places(offs[n2:-1], b.xn, b.xnr, b.xns, b.xnv)

        def fold_y():
            arrived(b.y1r, b.y1v)
            rows = fold(b.y1[x], b.y1r, nx - 1).astype(BF16)
            b.far[:, :, to_y:] = rows[:n2]
            b.near[...] = rows[n2:]
            to_places(offs[n2:-1], b.near, b.near_r, b.near_s, b.near_v)

        def fold_far():
            arrived(b.x1r, b.x1v)
            b.far[:, :, :to_y] = fold(b.x1[y], b.x1r, ny - 1).astype(BF16)
            to_places(offs[:n2], b.far, b.far_r, b.far_s, b.far_v)

        def fold_z():
            arrived(b.z1r, b.z1v)
            b.z2[:, :, to_y:] = fold(b.z1[x], b.z1r, nx - 1).astype(BF16)
            total = b.xn[n2 - 1]
            if n2 > 1:
                arrived(b.xnr, b.xnv)
                total = fold(total, b.xnr, n2 - 1)
            b.z2[:, :, :to_y] = total.astype(BF16)
            to_line("y", ny, y, b.z2, b.z2r, b.z2s, b.z2v)

        def drain():
            for copy in mine:
                copy.wait_send()
            mine.clear()

        def end_far():
            total = b.near[n2 - 1].astype(F32)
            if n2 > 1:
                arrived(b.near_r, b.near_v)
                total = fold(total, b.near_r, n2 - 1)
            arrived(b.far_r, b.far_v)
            b.fin[:, to_y:to_z] = fold(total, b.far_r.at[:, :, to_y:], n2)
            b.fin[:, :to_y] = fold(b.far_r[0, :, :to_y], b.far_r.at[1:, :, :to_y], n2 - 1)

        def end_z():
            arrived(b.z2r, b.z2v)
            total = fold(b.z2[y], b.z2r, ny - 1)
            b.fin[:, :to_y] = b.fin[:, :to_y] + total[:, :to_y]
            b.fin[:, to_z:] = total[:, to_y:]

        events = []

        def add(time, f, *args):
            events.append((time, functools.partial(f, *args)))

        ready = [2.2 + 0.5 * i for i in range(nz)]
        for i in range(nz):
            add(0.0 if i < 2 else ready[i - 2] + 0.2, own_product, i)
            add(ready[i], chip_product, i)
        for w in (0, 1):
            for p in (0, 1):
                half = ready[(p + 1) * n2 - 1] + 0.1
                for s in range(1, nx // 2 + 1):
                    add(half + 9.5 * (s - 1) + 0.1, hop, "x", p, w, s)
                for s in range(1, ny // 2 + 1):
                    add(half + 5.1 * (s - 1), hop, "y", p, w, s)
            for p in range(nx):
                begin = ready[0] + 0.1 if w == (0 if p < nx // 2 else 1) else ready[min(2, nz - 1)] + 0.1
                for s in range(1, nz // 2 + 1):
                    add(begin + 4.5 * (s - 1) + 0.01 * p, hop, "z", p, w, s)
        add(26.0, gather_xy)
        add(29.0, gather_z)
        add(29.2, gather_near)
        add(30.5, fold_y)
        add(33.0, fold_far)
        add(34.0, drain)
        add(35.0, fold_z)
        add(39.0, end_far)
        add(41.0, end_z)
        for _, step in sorted(events, key=lambda e: e[0]):
            step()

        keep = ROWS // 2
        send(b.fin.at[pl.ds((1 - core) * keep, keep)], b.fin_r, b.fin_s, b.fin_v, sibling)
        out_ref[:, pl.ds(pl.multiple_of(core * cols, TILE), cols)] = b.fin[pl.ds(core * keep, keep), :]
        arrived(b.fin_r, b.fin_v)
        out_ref[:, pl.ds(pl.multiple_of((1 - core) * cols, TILE), cols)] = b.fin_r[...]
        drain()

    for c in (0, 1):
        pl.when(core == c)(functools.partial(work, c))


def shards(t, acts, key_cot, value_cot):
    tokens, width = acts.shape
    cols = key_cot.shape[1]
    held = {(None, n): r for n, r in shared_buffers(t, tokens, width, cols).items()}
    for c, share in enumerate(SHARES):
        held.update({(c, n): r for n, r in core_buffers(t, *share).items()})
    anywhere = pl.BlockSpec(memory_space=pl.ANY)
    return pl.pallas_call(
        functools.partial(kernel, t, tuple(held)),
        out_shape=jax.ShapeDtypeStruct((ROWS // 2, 2 * cols), F32),
        in_specs=[anywhere] * 3,
        out_specs=pl.BlockSpec(memory_space=pltpu.VMEM),
        scratch_shapes=list(held.values()),
        compiler_params=pltpu.CompilerParams(
            collective_id=0, has_side_effects=True, vmem_limit_bytes=56 * 2**20
        ),
        cost_estimate=pl.CostEstimate(
            flops=4 * tokens * width * cols, bytes_accessed=2 * tokens * (width + 2 * cols),
            transcendentals=0,
        ),
    )(acts, key_cot, value_cot)


def solution(mesh):
    t = Torus(mesh.shape["node"], mesh.shape["local"], 4, 8)
    placed = P(("node", "local"), None)
    return jax.shard_map(
        functools.partial(shards, t), mesh=mesh, in_specs=(placed,) * 3,
        out_specs=placed, check_vma=False,
    )
```

```python
import functools
import types

import jax
import jax.numpy as jnp
from jax import lax
from jax.experimental import pallas as pl
from jax.experimental.pallas import tpu as pltpu
from jax.sharding import PartitionSpec as P

MESH = pl.DeviceIdType.MESH
F32, BF16 = jnp.float32, jnp.bfloat16
ROWS = 16
TILE = 128


class Torus:
    def __init__(self, n_node, n_local, nx, ny):
        self.nx, self.ny = nx, ny
        self.zh = n_node // nx
        self.zl = n_local // (2 * ny)
        self.nz = self.zh * self.zl

    def here(self):
        node, local = lax.axis_index("node"), lax.axis_index("local")
        x, zh = node // self.zh, node % self.zh
        zl, yc = local // (2 * self.ny), local % (2 * self.ny)
        return x, yc // 2, zh * self.zl + zl, yc % 2

    def device(self, x, y, z, core):
        return (
            x * self.zh + z // self.zl,
            ((z % self.zl) * self.ny + y) * 2 + core,
        )


def shared_buffers(t, tokens, width, cols):
    nx, nz = t.nx, t.nz
    dma = pltpu.SemaphoreType.DMA

    def held(*shape, dtype=BF16):
        return pltpu.VMEM(shape, dtype)

    return dict(
        acts=held(nx, tokens, width // nx), sib_acts=held(nx, tokens, width // nx),
        cot_own=held(tokens, cols), cot_give=held(tokens, cols), cot_sib=held(tokens, cols),
        first=held(nz, width // nz, cols, dtype=F32),
        fin=held(ROWS, cols, dtype=F32), fin_r=held(ROWS // 2, cols, dtype=F32),
        load_sem=dma((nx + 2,)), pair_s=dma((1 + nz,)), pair_v=dma((1 + nz,)),
        fin_s=dma(()), fin_v=dma(()),
    )


def core_buffers(t, xt, zt):
    nx, ny, nz = t.nx, t.ny, t.nz
    dma = pltpu.SemaphoreType.DMA
    n2, hx, hy, hz = nz // 2, nx // 2, ny // 2, nz // 2

    def slab(*shape, tiles=1):
        return pltpu.VMEM((*shape, ROWS, tiles * TILE), BF16)

    return dict(
        px=slab(nx, nz, ny, tiles=xt), py=slab(ny, nz, nx), pz=slab(nz, nx, ny, tiles=zt),
        rx=slab(2, 2, hx, n2, ny, tiles=xt), ry=slab(2, 2, hy, n2, nx), rz=slab(2, nx, hz, ny, tiles=zt),
        x1=slab(ny, n2, tiles=xt), x1r=slab(ny - 1, n2, tiles=xt),
        xn=slab(n2, ny, tiles=xt), xnr=slab(max(n2 - 1, 1), ny, tiles=xt),
        y1=slab(nx, nz), y1r=slab(nx - 1, nz),
        far=slab(n2, tiles=xt + 1), far_r=slab(n2, tiles=xt + 1), near=slab(n2), near_r=slab(max(n2 - 1, 1)),
        z1=slab(nx, ny, tiles=zt), z1r=slab(nx - 1, ny, tiles=zt), z2=slab(ny, tiles=zt + xt), z2r=slab(ny - 1, tiles=zt + xt),
        xs=dma((2, 2, hx)), xv=dma((2, 2, hx)), ys=dma((2, 2, hy)), yv=dma((2, 2, hy)),
        zs=dma((2, nx, hz)), zv=dma((2, nx, hz)),
        x1s=dma((ny - 1,)), x1v=dma(()), y1s=dma((nx - 1,)), y1v=dma(()), xns=dma((n2,)), xnv=dma(()),
        far_s=dma((n2,)), far_v=dma(()), near_s=dma((n2,)), near_v=dma(()),
        z1s=dma((nx - 1,)), z1v=dma(()), z2s=dma((ny - 1,)), z2v=dma(()),
    )


SHARES = ((2, 1), (1, 2))


def kernel(t, names, acts_hbm, key_hbm, value_hbm, out_ref, *refs):
    held = dict(zip(names, refs))
    b = types.SimpleNamespace(**{n: r for (c, n), r in held.items() if c is None})
    nx, ny, nz = t.nx, t.ny, t.nz
    x, y, z, core = t.here()
    tokens, width = acts_hbm.shape
    cols = key_hbm.shape[1]
    per_x = width // nx
    block = per_x // nz

    def wrap(v, n):
        return lax.rem(v + 2 * n, n)

    line = {("x", d): t.device(wrap(x + d, nx), y, z, core) for d in range(1, nx)}
    line.update({("y", d): t.device(x, wrap(y + d, ny), z, core) for d in range(1, ny)})
    line.update({("z", d): t.device(x, y, wrap(z + d, nz), core) for d in range(1, nz)})
    size = {"x": nx, "y": ny, "z": nz}

    def at(axis, d):
        return line[axis, d % size[axis]]

    sibling = t.device(x, y, z, 1 - core)

    def remote(src, dst, s, v, to):
        return pltpu.make_async_remote_copy(src, dst, s, v, device_id=to, device_id_type=MESH)

    started = []

    def send(src, dst, s, v, to):
        c = remote(src, dst, s, v, to)
        c.start()
        started.append(c)

    def arrived(buf, v):
        remote(buf, buf, v, v, sibling).wait_recv()

    barrier = pltpu.get_barrier_semaphore()
    peers = [sibling] + [line[a, d] for a, n in size.items() for d in sorted({1, n - 1})]
    for peer in peers:
        pl.semaphore_signal(barrier, inc=1, device_id=peer, device_id_type=MESH)

    n_load = nx

    @pl.when(core == 0)
    def _():
        pltpu.make_async_copy(key_hbm, b.cot_own, b.load_sem.at[n_load]).start()
        pltpu.make_async_copy(value_hbm, b.cot_give, b.load_sem.at[n_load + 1]).start()

    @pl.when(core == 1)
    def _():
        pltpu.make_async_copy(value_hbm, b.cot_own, b.load_sem.at[n_load]).start()
        pltpu.make_async_copy(key_hbm, b.cot_give, b.load_sem.at[n_load + 1]).start()

    loads = []
    for ix in range(nx):
        c = pltpu.make_async_copy(
            acts_hbm.at[:, pl.ds(ix * per_x, per_x)], b.acts.at[ix], b.load_sem.at[ix]
        )
        c.start()
        loads.append(c)

    pltpu.make_async_copy(key_hbm, b.cot_own, b.load_sem.at[n_load]).wait()
    pltpu.make_async_copy(key_hbm, b.cot_give, b.load_sem.at[n_load + 1]).wait()
    for c in loads:
        c.wait()
    pl.semaphore_wait(barrier, len(peers))

    offs = [nz // 2]
    for d in range(nz // 2 - 1, 0, -1):
        offs += [d, -d]
    offs.append(0)

    def cut(i):
        return pl.ds(pl.multiple_of(wrap(z + offs[i], nz) * block, TILE), block)

    send(b.cot_give, b.cot_sib, b.pair_s.at[0], b.pair_v.at[0], sibling)

    def give(i):
        part = (slice(None), slice(None), cut(i))
        return b.acts.at[part], b.sib_acts.at[part], b.pair_s.at[1 + i], b.pair_v.at[1 + i], sibling

    early = min(3, nz)
    for i in range(early):
        send(*give(i))

    def work(c):
        mine = list(started)

        def send(*args):
            copy = remote(*args)
            copy.start()
            mine.append(copy)

        b = types.SimpleNamespace(**{n: r for (of, n), r in held.items() if of in (None, c)})
        to_y = SHARES[c][0] * TILE
        to_z = to_y + TILE

        def dot(acts, i, cot):
            rows = jnp.concatenate([acts[ix, :, cut(i)] for ix in range(nx)], axis=1)
            return lax.dot_general(
                rows, cot[...], (((0,), (0,)), ((), ())), preferred_element_type=F32
            )

        def own_product(i):
            b.first[i] = dot(b.acts, i, b.cot_own)

        def chip_product(i):
            if i == 0:
                arrived(b.cot_sib, b.pair_v.at[0])
            arrived(b.sib_acts.at[:, :, cut(i)], b.pair_v.at[1 + i])
            rows = b.first[i] + dot(b.sib_acts, i, b.cot_sib)
            rows = rows.astype(BF16).reshape(nx, ny, ROWS, cols)
            b.px[:, i] = rows[..., :to_y]
            for ix in range(nx):
                b.py[:, i, ix] = rows[ix, :, :, to_y:to_z]
            b.pz[i] = rows[..., to_z:]

        n2 = nz // 2

        def ring(axis, p):
            half = pl.ds(p * n2, n2)
            if axis == "x":
                return (
                    nx, lambda d: b.px.at[wrap(x + d, nx), half], lambda w, q: b.rx.at[w, p, q],
                    lambda w, q: (b.xs.at[w, p, q], b.xv.at[w, p, q]), p,
                )
            if axis == "y":
                return (
                    ny, lambda d: b.py.at[wrap(y + d, ny), half], lambda w, q: b.ry.at[w, p, q],
                    lambda w, q: (b.ys.at[w, p, q], b.yv.at[w, p, q]), p,
                )
            return (
                nz, lambda d: b.pz.at[offs.index(n2 if d == -n2 else d), p], lambda w, q: b.rz.at[w, p, q],
                lambda w, q: (b.zs.at[w, p, q], b.zv.at[w, p, q]), 0 if p < nx // 2 else 1,
            )

        def count(n, w, long_way):
            return n // 2 if w == long_way else n // 2 - 1

        def hop(axis, p, w, s):
            n, sums, slot, sems, long_way = ring(axis, p)
            hops, way = count(n, w, long_way), 1 - 2 * w
            if s > hops:
                return
            chunk = sums(way * (hops - s + 1))
            if s > 1:
                arrived(slot(w, s - 2), sems(w, s - 2)[1])
                chunk[...] = (chunk[...].astype(F32) + slot(w, s - 2)[...].astype(F32)).astype(BF16)
            send(chunk, slot(w, s - 1), *sems(w, s - 1), at(axis, way))

        def gathered(axis, p):
            n, sums, slot, sems, long_way = ring(axis, p)
            total = sums(0)[...].astype(F32)
            for w in (0, 1):
                hops = count(n, w, long_way)
                if hops > 0:
                    arrived(slot(w, hops - 1), sems(w, hops - 1)[1])
                    total += slot(w, hops - 1)[...].astype(F32)
            return total.astype(BF16)

        def fold(mine, received, n):
            total = mine.astype(F32)
            for i in range(n):
                total += received[i].astype(F32)
            return total

        def to_line(axis, n, me, src, dst, ss, v):
            for d in range(1, n):
                send(src.at[wrap(me + d, n)], dst.at[d - 1], ss.at[d - 1], v, at(axis, d))

        def gather_xy():
            rows = gathered("x", 0)
            for g in range(n2):
                b.x1[:, g] = rows[g]
            for p in (1, 0):
                rows = gathered("y", p)
                for g in range(n2):
                    b.y1[:, p * n2 + g] = rows[g]
            to_line("y", ny, y, b.x1, b.x1r, b.x1s, b.x1v)
            to_line("x", nx, x, b.y1, b.y1r, b.y1s, b.y1v)

        def gather_z():
            for p in [*range(nx // 2, nx), *range(nx // 2)]:
                b.z1[p] = gathered("z", p)
            to_line("x", nx, x, b.z1, b.z1r, b.z1s, b.z1v)

        def to_places(places, src, dst, ss, v):
            for g, d in enumerate(places):
                send(src.at[g], dst.at[g], ss.at[g], v, at("z", d))

        def gather_near():
            b.xn[...] = gathered("x", 1)
            to_places(offs[n2:-1], b.xn, b.xnr, b.xns, b.xnv)

        def fold_y():
            arrived(b.y1r, b.y1v)
            rows = fold(b.y1[x], b.y1r, nx - 1).astype(BF16)
            b.far[:, :, to_y:] = rows[:n2]
            b.near[...] = rows[n2:]
            to_places(offs[n2:-1], b.near, b.near_r, b.near_s, b.near_v)

        def fold_far():
            arrived(b.x1r, b.x1v)
            b.far[:, :, :to_y] = fold(b.x1[y], b.x1r, ny - 1).astype(BF16)
            to_places(offs[:n2], b.far, b.far_r, b.far_s, b.far_v)

        def fold_z():
            arrived(b.z1r, b.z1v)
            b.z2[:, :, to_y:] = fold(b.z1[x], b.z1r, nx - 1).astype(BF16)
            total = b.xn[n2 - 1]
            if n2 > 1:
                arrived(b.xnr, b.xnv)
                total = fold(total, b.xnr, n2 - 1)
            b.z2[:, :, :to_y] = total.astype(BF16)
            to_line("y", ny, y, b.z2, b.z2r, b.z2s, b.z2v)

        def drain():
            for copy in mine:
                copy.wait_send()
            mine.clear()

        def end_far():
            total = b.near[n2 - 1].astype(F32)
            if n2 > 1:
                arrived(b.near_r, b.near_v)
                total = fold(total, b.near_r, n2 - 1)
            arrived(b.far_r, b.far_v)
            b.fin[:, to_y:to_z] = fold(total, b.far_r.at[:, :, to_y:], n2)
            b.fin[:, :to_y] = fold(b.far_r[0, :, :to_y], b.far_r.at[1:, :, :to_y], n2 - 1)

        def end_z():
            arrived(b.z2r, b.z2v)
            total = fold(b.z2[y], b.z2r, ny - 1)
            b.fin[:, :to_y] = b.fin[:, :to_y] + total[:, :to_y]
            b.fin[:, to_z:] = total[:, to_y:]

        events = []

        def add(time, f, *args):
            events.append((time, functools.partial(f, *args)))

        ready = [2.2 + 0.5 * i for i in range(nz)]
        for i in range(early, nz):
            add(0.1 + 0.25 * (i - early), lambda i: send(*give(i)), i)
        for i in range(nz):
            add(0.2 * i if i < 2 else ready[i - 2] + 0.2, own_product, i)
            add(ready[i], chip_product, i)
        for w in (0, 1):
            for p in (0, 1):
                half = ready[(p + 1) * n2 - 1] + 0.1
                for s in range(1, nx // 2 + 1):
                    add(half + (10.0 + 1.5 * p) * (s - 1) + 0.1, hop, "x", p, w, s)
                for s in range(1, ny // 2 + 1):
                    add(half + 5.1 * (s - 1), hop, "y", p, w, s)
            for p in range(nx):
                begin = ready[0] + 0.1 if w == (0 if p < nx // 2 else 1) else ready[min(2, nz - 1)] + 0.1
                for s in range(1, nz // 2 + 1):
                    add(begin + 4.5 * (s - 1) + 0.01 * p, hop, "z", p, w, s)
        add(26.0, gather_xy)
        add(29.0, gather_z)
        add(27.8, gather_near)
        add(30.5, fold_y)
        add(33.0, fold_far)
        add(32.8, drain)
        add(32.9, fold_z)
        add(39.0, end_far)
        add(41.0, end_z)
        for _, step in sorted(events, key=lambda e: e[0]):
            step()

        keep = ROWS // 2
        send(b.fin.at[pl.ds((1 - core) * keep, keep)], b.fin_r, b.fin_s, b.fin_v, sibling)
        out_ref[:, pl.ds(pl.multiple_of(core * cols, TILE), cols)] = b.fin[pl.ds(core * keep, keep), :]
        arrived(b.fin_r, b.fin_v)
        out_ref[:, pl.ds(pl.multiple_of((1 - core) * cols, TILE), cols)] = b.fin_r[...]
        drain()

    for c in (0, 1):
        pl.when(core == c)(functools.partial(work, c))


def shards(t, acts, key_cot, value_cot):
    tokens, width = acts.shape
    cols = key_cot.shape[1]
    held = {(None, n): r for n, r in shared_buffers(t, tokens, width, cols).items()}
    for c, share in enumerate(SHARES):
        held.update({(c, n): r for n, r in core_buffers(t, *share).items()})
    anywhere = pl.BlockSpec(memory_space=pl.ANY)
    return pl.pallas_call(
        functools.partial(kernel, t, tuple(held)),
        out_shape=jax.ShapeDtypeStruct((ROWS // 2, 2 * cols), F32),
        in_specs=[anywhere] * 3,
        out_specs=pl.BlockSpec(memory_space=pltpu.VMEM),
        scratch_shapes=list(held.values()),
        compiler_params=pltpu.CompilerParams(
            collective_id=0, has_side_effects=True, vmem_limit_bytes=56 * 2**20
        ),
        cost_estimate=pl.CostEstimate(
            flops=4 * tokens * width * cols, bytes_accessed=2 * tokens * (width + 2 * cols),
            transcendentals=0,
        ),
    )(acts, key_cot, value_cot)


def solution(mesh):
    t = Torus(mesh.shape["node"], mesh.shape["local"], 4, 8)
    placed = P(("node", "local"), None)
    return jax.shard_map(
        functools.partial(shards, t), mesh=mesh, in_specs=(placed,) * 3,
        out_specs=placed, check_vma=False,
    )
```
